32 devices in a mesh: section: 2 (over core), dp: 16 (over z, y, x).
Axes of the slice: x: 2, y: 2, z: 4, core: 2. Of those that a mesh axis runs over, the one named last changes fastest.
Arguments:
- patches: bfloat16 [2, 6400, 768], P('section', 'dp'), may hold values from -6 to 6
- pos_table: float32 [198, 768], replicated, may hold values from -3 to 3
- pos_index: int32 [2, 6400], P(None, 'dp'), may hold values from 0 to 197
- image_ids: int32 [2, 6400], P(None, 'dp'), may hold values from 0 to 4, as said below
- ln_gains: float32 [2, 2, 768], P('section'), may hold values from 0.5 to 1.5
- biases: float32 [2, 6, 768], P('section'), may hold values from -2 to 2
- w_qkv: bfloat16 [2, 768, 2304], P('section'), may hold values from -0.21875 to 0.21875
- w_out: bfloat16 [2, 768, 768], P('section'), may hold values from -0.875 to 0.875
- w_fc1: bfloat16 [2, 768, 3072], P('section'), may hold values from -0.21875 to 0.21875
- b_fc1: float32 [2, 3072], P('section'), may hold values from -2 to 2
- w_fc2: bfloat16 [2, 3072, 768], P('section'), may hold values from -0.109375 to 0.109375
- cotangent: bfloat16 [2, 6400, 768], P('section', 'dp'), may hold values from -6 to 6
Outputs:
- out_tokens: bfloat16 [2, 6400, 768], P('section', 'dp')
- grad_patches: bfloat16 [2, 6400, 768], P('section', 'dp')
- grad_table: float32 [198, 768], P(None, ('section', 'dp'))
- grad_gains: float32 [2, 2, 768], P('section', None, 'dp')
- grad_biases: float32 [2, 6, 768], P('section', None, 'dp')
- grad_w_qkv: float32 [2, 768, 2304], P('section', 'dp')
- grad_w_out: float32 [2, 768, 768], P('section', 'dp')
- grad_w_fc1: float32 [2, 768, 3072], P('section', 'dp')
- grad_b_fc1: float32 [2, 3072], P('section', 'dp')
- grad_w_fc2: float32 [2, 3072, 768], P('section', 'dp')
The draws below stay inside these ranges and needn't reach their ends.
Inputs may be any that keep to these rules, and one draw needn't show every extreme that they name: `image_ids`: each block of 400 tokens is packed in one of three ways: one image of 394 tokens; two images of 134 tokens and one of 69; or one of 134 and three of 69, in an order that varies. Each image is a contiguous run numbered by its place in the block from 0, and the remaining tokens at the block's end form one more run with the next number. Every draw holds blocks of the first and the third kind.
All inputs are finite; a program needn't handle non-finite values.
Results may differ from the reference program's by a relative error of at most 0.015.
Values may be sent and summed in bfloat16 or wider, within the bound.
No kernel may reach another device: no remote copies, remote signals or barrier semaphores. Data moves between devices by JAX's collectives and lax.ppermute only.
A program may use at most 320 MiB of HBM per device.

```python
import jax
import jax.numpy as jnp
from jax import lax

D = 768
HEAD = 64
FF = 3072
POS = 198
ROWS = 400
MB = 2
MOST = 394
MID_LEN = 134
SMALL_LEN = 69
TOKENS = 6400
N_SECTION = 2


def draw_image_ids(key, part):
    key = jax.random.fold_in(key, 7)
    buffers = MB * (TOKENS // ROWS)
    kind_key, order_key = jax.random.split(key)
    kinds = jax.random.randint(kind_key, (buffers,), 0, 3).astype(jnp.int32)
    block_number = jnp.arange(buffers, dtype=jnp.int32)
    kinds = jnp.where(block_number == 0, 0, jnp.where(block_number == 1, 2, kinds)).astype(jnp.int32)
    orders = jax.random.randint(order_key, (buffers,), 0, 3).astype(jnp.int32)
    pad_one = ROWS - MOST
    pad_two = ROWS - 2 * MID_LEN - SMALL_LEN
    pad_three = ROWS - MID_LEN - 3 * SMALL_LEN
    table = jnp.array([[[MOST, pad_one, 0, 0, 0], [MOST, pad_one, 0, 0, 0], [MOST, pad_one, 0, 0, 0]], [[MID_LEN, MID_LEN, SMALL_LEN, pad_two, 0], [MID_LEN, SMALL_LEN, MID_LEN, pad_two, 0], [SMALL_LEN, MID_LEN, MID_LEN, pad_two, 0]], [[MID_LEN, SMALL_LEN, SMALL_LEN, SMALL_LEN, pad_three], [SMALL_LEN, MID_LEN, SMALL_LEN, SMALL_LEN, pad_three], [SMALL_LEN, SMALL_LEN, MID_LEN, SMALL_LEN, pad_three]]], dtype=jnp.int32)
    lengths = table[kinds, orders]
    bounds = jnp.cumsum(lengths, axis=1)
    positions = jnp.arange(ROWS, dtype=jnp.int32)
    image_rows = jnp.sum((positions[None, :, None] >= bounds[:, None, :4]).astype(jnp.int32), axis=2)
    return image_rows.reshape(MB, TOKENS).astype(jnp.int32)


def touch_ends(drawn, rng, smallest, high):
    index_at = [jax.random.randint(jax.random.fold_in(rng, axis), (), 0, length) for axis, length in enumerate(drawn.shape)]
    main_axis = drawn.shape.index(max(drawn.shape))
    neighbour = index_at[:main_axis] + [(index_at[main_axis] + 1) % drawn.shape[main_axis]] + index_at[main_axis + 1:]
    return drawn.at[tuple(index_at)].set(smallest).at[tuple(neighbour)].set(high)


def shard_levels(key, dims, cuts, smallest, largest):
    gain = 1.0
    for dim, blocks in cuts:
        draws = jax.random.uniform(jax.random.fold_in(jax.random.fold_in(key, 6), dim), (blocks,), jnp.float32, smallest / len(cuts), largest / len(cuts))
        gain = gain * jnp.repeat(jnp.exp(draws), dims[dim] // blocks).reshape((-1,) + (1,) * (len(dims) - 1 - dim))
    return gain


def centred(rng, extent, scale, limit, cuts=(), kind=jnp.bfloat16):
    values = jax.random.normal(rng, extent, jnp.float32) * scale
    if len(cuts) > 0:
        values = shard_levels(rng, extent, cuts, -0.22, 0.18) * values
    return jnp.clip(values, min=-limit, max=limit).astype(kind)


def setup_inputs(seed: int = 0) -> dict:
    key_list = jax.random.split(jax.random.key(seed), 13)
    return {
        "patches": centred(key_list[0], (MB, TOKENS, D), 1.0, 6.0, ((0, 2), (1, 16))),
        "pos_table": centred(key_list[1], (POS, D), 0.5, 3.0, (), jnp.float32),
        "pos_index": touch_ends(jax.random.randint(key_list[2], (MB, TOKENS), 0, POS), jax.random.fold_in(key_list[2], 1), 0, POS - 1).astype(jnp.int32),
        "image_ids": draw_image_ids(jax.random.fold_in(key_list[12], 71), 0),
        "ln_gains": jnp.clip(1.0 + 0.1 * jax.random.normal(key_list[4], (N_SECTION, 2, D), jnp.float32), 0.5, 1.5),
        "biases": centred(key_list[5], (N_SECTION, 6, D), 0.3, 2.0, ((0, 2),), jnp.float32),
        "w_qkv": centred(key_list[6], (N_SECTION, D, 3 * D), D ** -0.5, 0.21875, ((0, 2),)),
        "w_out": centred(key_list[7], (N_SECTION, D, D), (D // 16) ** -0.5, 0.875, ((0, 2),)),
        "w_fc1": centred(key_list[8], (N_SECTION, D, FF), D ** -0.5, 0.21875, ((0, 2),)),
        "b_fc1": centred(key_list[9], (N_SECTION, FF), 0.3, 2.0, ((0, 2),), jnp.float32),
        "w_fc2": centred(key_list[10], (N_SECTION, FF, D), FF ** -0.5, 0.109375, ((0, 2),)),
        "cotangent": centred(key_list[11], (MB, TOKENS, D), 1.0, 6.0, ((0, 2), (1, 16))),
    }


@jax.custom_vjp
def low(v):
    return lax.optimization_barrier(v.astype(jnp.bfloat16)).astype(jnp.float32)

@jax.custom_vjp
def low_back(v):
    return v

def low_keep(v):
    return (low(v), None)

def low_pass(kept, grad):
    return (grad,)

def back_keep(v):
    return (v, None)

def back_low(kept, grad):
    return (low(grad),)
low.defvjp(low_keep, low_pass)
low_back.defvjp(back_keep, back_low)
eps_norm = 1e-06
neg_large = -1e+30

def normalize(values, gain_vec, shift_vec):
    center = values - lax.optimization_barrier(jnp.mean(values, axis=-1, keepdims=True))
    variance = lax.optimization_barrier(jnp.mean(center * center, axis=-1, keepdims=True))
    return center * lax.rsqrt(variance + eps_norm) * gain_vec + shift_vec

def matmul(left, right):
    return jnp.dot(left, right, precision=lax.Precision.HIGHEST, preferred_element_type=jnp.float32)

def block_forward(inputs, same_image, gains, shifts, w_qkv, w_out, w_fc1, b_fc1, w_fc2):
    row_count, model_width = inputs.shape
    head_count = model_width // HEAD
    attn_in = low(normalize(inputs, gains[0], shifts[0]))
    qkv_bias = jnp.concatenate([shifts[1], jnp.zeros_like(shifts[1]), shifts[2]])
    qkv = low(low_back(matmul(attn_in, w_qkv) + qkv_bias))
    queries = qkv[:, :model_width].reshape(row_count, head_count, HEAD)
    key_rows = qkv[:, model_width:2 * model_width].reshape(row_count, head_count, HEAD)
    value_rows = qkv[:, 2 * model_width:].reshape(row_count, head_count, HEAD)
    scores = jnp.einsum('qhd,khd->hqk', queries, key_rows, precision=lax.Precision.HIGHEST)
    scores = low_back(scores * HEAD ** (-0.5))
    scores = jnp.where(same_image[None], scores, neg_large)
    attn_probs = low(jax.nn.softmax(scores, axis=-1))
    context = jnp.einsum('hqk,khd->qhd', attn_probs, value_rows, precision=lax.Precision.HIGHEST)
    context = low(low_back(context.reshape(row_count, model_width)))
    residual = inputs + low_back(matmul(context, w_out) + shifts[3])
    mlp_in = low(normalize(residual, gains[1], shifts[4]))
    hidden = low_back(matmul(mlp_in, w_fc1) + b_fc1)
    active = low(jax.nn.gelu(hidden, approximate=False))
    return residual + low_back(matmul(active, w_fc2) + shifts[5])

def network(rows_in, table, weights, positions, same_image):
    hidden = rows_in + table[positions]
    hidden = block_forward(hidden, same_image, *[item[0] for item in weights])
    hidden = low(low_back(hidden))
    return block_forward(hidden, same_image, *[item[1] for item in weights])

def reference(patches, pos_table, pos_index, image_ids, ln_gains, biases, w_qkv, w_out, w_fc1, b_fc1, w_fc2, cotangent):
    weights = tuple((item.astype(jnp.float32) for item in (ln_gains, biases, w_qkv, w_out, w_fc1, b_fc1, w_fc2)))
    table = pos_table.astype(jnp.float32)
    buffers = MB * (TOKENS // ROWS)
    rows_in = patches.astype(jnp.float32).reshape(buffers, ROWS, D)
    grads_in = cotangent.astype(jnp.float32).reshape(buffers, ROWS, D)
    positions = pos_index.reshape(buffers, ROWS).astype(jnp.int32)
    image_rows = image_ids.reshape(buffers, ROWS).astype(jnp.int32)

    def buffer_step(totals, buffer):
        rows_blk, grad_blk, pos_blk, image_blk = buffer
        same_image = image_blk[:, None] == image_blk[None, :]
        result, pullback = jax.vjp(lambda rows_arg, table_arg, weights_arg: network(rows_arg, table_arg, weights_arg, pos_blk, same_image), rows_blk, table, weights)
        grad_rows, grad_tab, grad_weights = pullback(grad_blk)
        totals = jax.tree.map(lambda left, right: left + right, totals, (grad_tab, grad_weights))
        return (totals, (result.astype(jnp.bfloat16), grad_rows.astype(jnp.bfloat16)))
    initial = jax.tree.map(jnp.zeros_like, (table, weights))
    totals, stacked = lax.scan(buffer_step, initial, (rows_in, grads_in, positions, image_rows))
    grad_tab, grad_weights = totals
    outputs, grad_rows = stacked
    return (outputs.reshape(MB, TOKENS, D), grad_rows.reshape(MB, TOKENS, D), grad_tab, grad_weights[0], grad_weights[1], grad_weights[2], grad_weights[3], grad_weights[4], grad_weights[5], grad_weights[6])
```

```python
import jax
import jax.numpy as jnp
from jax import lax
from jax.sharding import PartitionSpec as P

HEADS = 12
HEAD = 64


eps_norm = 1e-06
neg_large = -1e30
inv_sqrt_two = 0.7071067811865476
inv_sqrt_tau = 0.3989422804014327


def passed_along(array, axis, by):
    devices = lax.axis_size(axis)
    pairs = [(i, i + by) for i in range(devices) if 0 <= i + by < devices]
    return lax.ppermute(array, axis, pairs)


def from_partner(block, axis, apart):
    count = lax.axis_size(axis)
    route = []
    for low in range(count):
        high = low | 1 << apart
        if high != low and high < count:
            route += [(low, high), (high, low)]
    return lax.ppermute(block, axis, route)


def normalize(values, gain_vec, shift_vec):
    center = values - jnp.mean(values, axis=-1, keepdims=True)
    inverse = lax.rsqrt(jnp.mean(center * center, axis=-1, keepdims=True) + eps_norm)
    normed = center * inverse
    return (normed * gain_vec + shift_vec, normed, inverse)


def normalize_back(grad_out, normed, inverse, gain_vec):
    grad_norm = grad_out * gain_vec
    grad_in = inverse * (
        grad_norm
        - jnp.mean(grad_norm, axis=-1, keepdims=True)
        - normed * jnp.mean(grad_norm * normed, axis=-1, keepdims=True)
    )
    return (grad_in, jnp.sum(grad_out * normed, axis=0), jnp.sum(grad_out, axis=0))


def split_groups(matrix):
    return matrix.reshape(matrix.shape[0], HEADS // 4, 4 * HEAD).transpose(1, 0, 2)


def join_groups(stacked):
    return stacked.transpose(1, 0, 2).reshape(stacked.shape[1], -1)


def group_scores(queries, key_rows, same_image):
    row_count = queries.shape[0]
    query_heads = queries.reshape(row_count, 4, HEAD)
    key_heads = key_rows.reshape(row_count, 4, HEAD)
    scores = jnp.einsum(
        "qhd,khd->hqk", query_heads, key_heads, preferred_element_type=jnp.float32
    ) * HEAD ** (-0.5)
    return jnp.where(same_image[None], scores, neg_large)


def attend_group(operands, same_image):
    queries, key_rows, value_rows = operands
    row_count = queries.shape[0]
    scores = group_scores(queries, key_rows, same_image)
    row_peak = jnp.max(scores, axis=-1, keepdims=True)
    shifted = jnp.exp(scores - row_peak)
    row_total = jnp.sum(shifted, axis=-1, keepdims=True)
    attn_probs = (shifted / row_total).astype(jnp.bfloat16)
    value_heads = value_rows.reshape(row_count, 4, HEAD)
    context = jnp.einsum(
        "hqk,khd->qhd", attn_probs, value_heads, preferred_element_type=jnp.float32
    )
    return (context.reshape(row_count, 4 * HEAD), (row_peak + jnp.log(row_total))[..., 0])


def attend(qkv, same_image):
    model_width = qkv.shape[1] // 3
    operands = (
        split_groups(qkv[:, :model_width]),
        split_groups(qkv[:, model_width : 2 * model_width]),
        split_groups(qkv[:, 2 * model_width :]),
    )
    context, log_total = lax.map(lambda group: attend_group(group, same_image), operands)
    return (join_groups(context), log_total)


def attend_group_back(operands, same_image):
    queries, key_rows, value_rows, log_total, grad_context = operands
    row_count = queries.shape[0]
    scores = group_scores(queries, key_rows, same_image)
    attn_probs = jnp.exp(scores - log_total[..., None])
    query_heads = queries.reshape(row_count, 4, HEAD)
    key_heads = key_rows.reshape(row_count, 4, HEAD)
    value_heads = value_rows.reshape(row_count, 4, HEAD)
    grad_heads = grad_context.reshape(row_count, 4, HEAD)
    grad_values = jnp.einsum(
        "hqk,qhd->khd",
        attn_probs.astype(jnp.bfloat16),
        grad_heads,
        preferred_element_type=jnp.float32,
    )
    grad_probs = jnp.einsum(
        "qhd,khd->hqk", grad_heads, value_heads, preferred_element_type=jnp.float32
    )
    grad_scores = (
        attn_probs * (grad_probs - jnp.sum(attn_probs * grad_probs, axis=-1, keepdims=True))
    ).astype(jnp.bfloat16)
    grad_queries = jnp.einsum(
        "hqk,khd->qhd", grad_scores, key_heads, preferred_element_type=jnp.float32
    ) * HEAD ** (-0.5)
    grad_keys = jnp.einsum(
        "hqk,qhd->khd", grad_scores, query_heads, preferred_element_type=jnp.float32
    ) * HEAD ** (-0.5)
    return (
        grad_queries.reshape(row_count, 4 * HEAD),
        grad_keys.reshape(row_count, 4 * HEAD),
        grad_values.reshape(row_count, 4 * HEAD),
    )


def attend_back(qkv, log_total, grad_context, same_image):
    model_width = qkv.shape[1] // 3
    operands = (
        split_groups(qkv[:, :model_width]),
        split_groups(qkv[:, model_width : 2 * model_width]),
        split_groups(qkv[:, 2 * model_width :]),
        log_total,
        split_groups(grad_context),
    )
    grad_queries, grad_keys, grad_values = lax.map(
        lambda group: attend_group_back(group, same_image), operands
    )
    return jnp.concatenate(
        [join_groups(grad_queries), join_groups(grad_keys), join_groups(grad_values)], axis=1
    )


def layer_forward(inputs, same_image, params):
    gains, shifts, w_qkv, w_out, w_fc1, b_fc1, w_fc2 = params
    attn_in = normalize(inputs, gains[0], shifts[0])[0].astype(jnp.bfloat16)
    qkv_bias = jnp.concatenate([shifts[1], jnp.zeros_like(shifts[1]), shifts[2]])
    qkv = (jnp.dot(attn_in, w_qkv, preferred_element_type=jnp.float32) + qkv_bias).astype(
        jnp.bfloat16
    )
    context, log_total = attend(qkv, same_image)
    context = context.astype(jnp.bfloat16)
    residual = inputs + (jnp.dot(context, w_out, preferred_element_type=jnp.float32) + shifts[3])
    mlp_in = normalize(residual, gains[1], shifts[4])[0].astype(jnp.bfloat16)
    hidden = jnp.dot(mlp_in, w_fc1, preferred_element_type=jnp.float32) + b_fc1
    active = jax.nn.gelu(hidden, approximate=False).astype(jnp.bfloat16)
    result = residual + (jnp.dot(active, w_fc2, preferred_element_type=jnp.float32) + shifts[5])
    return (result, (inputs, attn_in, qkv, log_total, context, residual, mlp_in, hidden, active))


def layer_backward(grad_out, stashed, same_image, params):
    gains, shifts, w_qkv, w_out, w_fc1, b_fc1, w_fc2 = params
    inputs, attn_in, qkv, log_total, context, residual, mlp_in, hidden, active = stashed
    model_width = inputs.shape[1]
    grad_branch = grad_out.astype(jnp.bfloat16)
    grad_w_fc2 = jnp.einsum("rf,rd->fd", active, grad_branch, preferred_element_type=jnp.float32)
    grad_b_fc2 = jnp.sum(grad_branch.astype(jnp.float32), axis=0)
    grad_active = jnp.dot(grad_branch, w_fc2.T, preferred_element_type=jnp.float32)
    gate_slope = (
        0.5 * (1.0 + lax.erf(hidden * inv_sqrt_two))
        + hidden * jnp.exp(-0.5 * hidden * hidden) * inv_sqrt_tau
    )
    grad_hidden = (grad_active * gate_slope).astype(jnp.bfloat16)
    grad_w_fc1 = jnp.einsum("rd,rf->df", mlp_in, grad_hidden, preferred_element_type=jnp.float32)
    grad_b_fc1 = jnp.sum(grad_hidden.astype(jnp.float32), axis=0)
    grad_mlp_in = jnp.dot(grad_hidden, w_fc1.T, preferred_element_type=jnp.float32)
    _, normed_mid, inverse_mid = normalize(residual, gains[1], shifts[4])
    grad_mid, grad_gain_mid, grad_shift_mid = normalize_back(
        grad_mlp_in, normed_mid, inverse_mid, gains[1]
    )
    grad_residual = grad_out + grad_mid
    grad_attn_out = grad_residual.astype(jnp.bfloat16)
    grad_w_out = jnp.einsum("ra,rd->ad", context, grad_attn_out, preferred_element_type=jnp.float32)
    grad_b_out = jnp.sum(grad_attn_out.astype(jnp.float32), axis=0)
    grad_context = jnp.dot(grad_attn_out, w_out.T, preferred_element_type=jnp.float32).astype(
        jnp.bfloat16
    )
    grad_qkv = attend_back(qkv, log_total, grad_context, same_image).astype(jnp.bfloat16)
    grad_w_qkv = jnp.einsum("rd,rc->dc", attn_in, grad_qkv, preferred_element_type=jnp.float32)
    grad_bias_qkv = jnp.sum(grad_qkv.astype(jnp.float32), axis=0)
    grad_attn_in = jnp.dot(grad_qkv, w_qkv.T, preferred_element_type=jnp.float32)
    _, normed_in, inverse_in = normalize(inputs, gains[0], shifts[0])
    grad_norm_in, grad_gain_in, grad_shift_in = normalize_back(
        grad_attn_in, normed_in, inverse_in, gains[0]
    )
    grad_inputs = grad_residual + grad_norm_in
    grad_gains = jnp.stack([grad_gain_in, grad_gain_mid])
    grad_shifts = jnp.stack(
        [
            grad_shift_in,
            grad_bias_qkv[:model_width],
            grad_bias_qkv[2 * model_width :],
            grad_b_out,
            grad_shift_mid,
            grad_b_fc2,
        ]
    )
    return (
        grad_inputs,
        (grad_gains, grad_shifts, grad_w_qkv, grad_w_out, grad_w_fc1, grad_b_fc1, grad_w_fc2),
    )


def run_forward(inputs, same_image, params):
    result, stashed = layer_forward(inputs, same_image, params)
    return (result, stashed)


def run_backward(grad_out, stashed, same_image, params):
    return layer_backward(grad_out, stashed, same_image, params)


def only_when(condition, compute):
    return lax.cond(condition, compute, lambda: jax.tree.map(jnp.zeros_like, compute()))


def send_onward(values):
    return passed_along(values.astype(jnp.bfloat16), "section", 1)


def send_backward(values):
    return passed_along(values.astype(jnp.bfloat16), "section", -1)


def per_device(
    patches,
    pos_table,
    pos_index,
    image_ids,
    ln_gains,
    biases,
    w_qkv,
    w_out,
    w_fc1,
    b_fc1,
    w_fc2,
    cotangent,
):
    lead_section = lax.axis_index("section") == 0
    params = (ln_gains[0], biases[0], w_qkv[0], w_out[0], w_fc1[0], b_fc1[0], w_fc2[0])
    own_rows = patches[0]
    own_grad = cotangent[0]
    incoming = from_partner(jnp.where(lead_section, own_grad, own_rows), "section", 0)
    image_masks = [
        image_ids[index_micro][:, None] == image_ids[index_micro][None, :]
        for index_micro in range(2)
    ]
    table_rows = pos_table.shape[0]

    def one_hot(index_micro):
        return (
            pos_index[index_micro][:, None] == jnp.arange(table_rows, dtype=jnp.int32)[None, :]
        ).astype(jnp.float32)

    def embed_rows(index_micro, rows_in):
        return rows_in.astype(jnp.float32) + jnp.dot(
            one_hot(index_micro), pos_table, precision=lax.Precision.HIGHEST
        )

    out_first, stash_first = only_when(
        lead_section, lambda: run_forward(embed_rows(0, own_rows), image_masks[0], params)
    )
    arrived = send_onward(out_first)
    second_in = jnp.where(lead_section, embed_rows(1, incoming), arrived.astype(jnp.float32))
    second_mask = jnp.where(lead_section, image_masks[1], image_masks[0])
    out_second, stash_second = run_forward(second_in, second_mask, params)
    arrived_next = send_onward(out_second)

    def tail_work():
        out_third, stash_third = run_forward(
            arrived_next.astype(jnp.float32), image_masks[1], params
        )
        grad_third, grads_third = run_backward(
            incoming.astype(jnp.float32), stash_second, image_masks[0], params
        )
        return (out_third, stash_third, grad_third, grads_third)

    out_third, stash_third, grad_third, grads_third = only_when(
        jnp.logical_not(lead_section), tail_work
    )
    returned_first = send_backward(grad_third)
    middle_grad_in = jnp.where(
        lead_section, returned_first.astype(jnp.float32), own_grad.astype(jnp.float32)
    )
    middle_stash = jax.tree.map(
        lambda left, right: jnp.where(lead_section, left, right), stash_first, stash_third
    )
    middle_mask = jnp.where(lead_section, image_masks[0], image_masks[1])
    grad_fourth, grads_fourth = run_backward(middle_grad_in, middle_stash, middle_mask, params)
    returned_second = send_backward(grad_fourth)
    grad_fifth, grads_fifth = only_when(
        lead_section,
        lambda: run_backward(
            returned_second.astype(jnp.float32), stash_second, image_masks[1], params
        ),
    )
    leaving = jnp.where(lead_section, grad_fifth, out_second).astype(jnp.bfloat16)
    returned = from_partner(leaving, "section", 0)
    out_tokens = jnp.where(lead_section, returned, out_third.astype(jnp.bfloat16))
    grad_patches = jnp.where(lead_section, grad_fourth.astype(jnp.bfloat16), returned)
    table_term = jnp.dot(one_hot(0).T, grad_fourth, precision=lax.Precision.HIGHEST) + jnp.dot(
        one_hot(1).T, grad_fifth, precision=lax.Precision.HIGHEST
    )
    table_term = jnp.where(lead_section, table_term, 0.0)
    totals = jax.tree.map(
        lambda left, middle, right: left + middle + right, grads_third, grads_fourth, grads_fifth
    )
    return (out_tokens[None], grad_patches[None]) + scatter_sums(totals, table_term)


def halving_order(bits, first):
    order = list(range(bits))
    if bits == 4:
        order = [0, 2, 1, 3]
    swap = {0: first, first: 0}
    return [swap.get(bit, bit) for bit in order]


def scatter_blocks(blocks, order):
    count = blocks.shape[0]
    bits = count.bit_length() - 1
    rest = blocks.shape[1:]
    place = lax.axis_index("dp")
    held = blocks.reshape((2,) * bits + rest)
    left = list(reversed(range(bits)))
    for bit in order:
        dim = left.index(bit)
        mine = (place >> bit) & 1
        away = lax.dynamic_index_in_dim(held, 1 - mine, dim, keepdims=False)
        kept = lax.dynamic_index_in_dim(held, mine, dim, keepdims=False)
        route = [(i, i ^ (1 << bit)) for i in range(count)]
        came = lax.ppermute(away, "dp", route)
        held = (kept.astype(jnp.float32) + came.astype(jnp.float32)).astype(blocks.dtype)
        left.remove(bit)
    return held


def scatter_sums(totals, table_term):
    count = lax.axis_size("dp")
    bits = count.bit_length() - 1
    orders = (halving_order(bits, 0), halving_order(bits, 1))
    gains, shifts, w_qkv, w_out, w_fc1, b_fc1, w_fc2 = totals
    width = gains.shape[1]

    def big(grad):
        rows = grad.shape[0] // count
        blocks = grad.astype(jnp.bfloat16).reshape(count, rows, grad.shape[1])
        half = grad.shape[1] // 2
        parts = [
            scatter_blocks(blocks[..., :half], orders[0]),
            scatter_blocks(blocks[..., half:], orders[1]),
        ]
        return jnp.concatenate(parts, axis=-1).astype(jnp.float32)

    table_rows = table_term.shape[0]
    sections = lax.axis_size("section")
    table = table_term.reshape(table_rows, sections, count, -1).transpose(2, 1, 0, 3)
    columns = table.shape[-1]
    pieces = [
        table.reshape(count, -1),
        gains.reshape(2, count, -1).transpose(1, 0, 2).reshape(count, -1),
        shifts.reshape(6, count, -1).transpose(1, 0, 2).reshape(count, -1),
        b_fc1.reshape(count, -1),
    ]
    sizes = [piece.shape[1] for piece in pieces]
    flat = scatter_blocks(jnp.concatenate(pieces, axis=1), orders[0])
    bounds = [sum(sizes[:i]) for i in range(5)]
    parts = [flat[bounds[i] : bounds[i + 1]] for i in range(4)]
    table = parts[0].reshape(sections, table_rows, columns)
    arrived = lax.ppermute(table[1], "section", [(0, 1)])
    lead_section = lax.axis_index("section") == 0
    table = jnp.where(lead_section, table[0], arrived)
    return (
        table,
        parts[1].reshape(2, -1)[None],
        parts[2].reshape(6, -1)[None],
        big(w_qkv)[None],
        big(w_out)[None],
        big(w_fc1)[None],
        parts[3][None],
        big(w_fc2)[None],
    )


def solution(mesh):
    placed = (
        P("section", "dp", None),
        P(),
        P(None, "dp"),
        P(None, "dp"),
        P("section", None, None),
        P("section", None, None),
        P("section", None, None),
        P("section", None, None),
        P("section", None, None),
        P("section", None),
        P("section", None, None),
        P("section", "dp", None),
    )
    return jax.shard_map(
        per_device,
        mesh=mesh,
        in_specs=placed,
        out_specs=(
            P("section", "dp", None),
            P("section", "dp", None),
            P(None, ("section", "dp")),
            P("section", None, "dp"),
            P("section", None, "dp"),
            P("section", "dp", None),
            P("section", "dp", None),
            P("section", "dp", None),
            P("section", "dp"),
            P("section", "dp", None),
        ),
        check_vma=False,
    )
```

```python
import types

import jax
import jax.numpy as jnp
from jax import lax
from jax.experimental import pallas as pl
from jax.experimental.pallas import tpu as pltpu
from jax.sharding import PartitionSpec as P

HEAD = 64
PAIR = 2 * HEAD
TILE = 256
eps_norm = 1e-06
neg_large = -1e30
f32, bf16 = jnp.float32, jnp.bfloat16
NN = (((1,), (0,)), ((), ()))
NT = (((1,), (1,)), ((), ()))
TN = (((0,), (0,)), ((), ()))
FLOPS_PER_US = 11_500_000_000
VMEM = 62 * 2**20


def dot(left, right, dims=NN):
    return lax.dot_general(left, right, dims, preferred_element_type=f32)


def struct(pair):
    return jax.ShapeDtypeStruct(*pair)


def call(body, us, sel, small, large, outs, scratch, copies=40, after=()):
    names, operands = [], []
    for name, value in (small | large).items():
        parts = value if isinstance(value, (tuple, list)) else (value,)
        names.append((name, len(parts), isinstance(value, (tuple, list))))
        operands += list(parts)
    operands += list(after)
    n_small = sum(len(v) if isinstance(v, (tuple, list)) else 1 for v in small.values())

    def kernel(sel_ref, *refs):
        refs = list(refs)
        r = types.SimpleNamespace(sel=sel_ref)
        for name, length, several in names:
            taken = [refs.pop(0) for _ in range(length)]
            setattr(r, name, taken if several else taken[0])
        del refs[: len(after)]
        for name in list(outs) + list(scratch):
            setattr(r, name, refs.pop(0))
        sems = refs.pop(0)
        begun, used = [], []

        def semaphore():
            used.append(0)
            return sems.at[len(used) - 1]

        def get(src, dst):
            copy = pltpu.make_async_copy(src, dst, semaphore())
            copy.start()
            return copy

        def pick(pair, dst):
            sem = semaphore()

            @pl.when(r.sel[0] != 0)
            def _():
                pltpu.make_async_copy(pair[0], dst, sem).start()

            @pl.when(r.sel[0] == 0)
            def _():
                pltpu.make_async_copy(pair[1], dst, sem).start()

            return pltpu.make_async_copy(pair[0], dst, sem)

        def pieces(pair, dst, count, axis):
            step = dst.shape[axis] // count
            cuts = [pl.ds(i * step, step) for i in range(count)]
            cuts = [(cut,) if axis == 0 else (slice(None), cut) for cut in cuts]
            return [pick([ref.at[cut] for ref in pair], dst.at[cut]) for cut in cuts]

        r.get, r.pick, r.pieces = get, pick, pieces
        r.put = lambda src, dst: begun.append(get(src, dst))
        r.either = lambda pair: jnp.where(r.sel[0] != 0, pair[0][...], pair[1][...])
        body(r)
        for copy in begun:
            copy.wait()

    here = pl.BlockSpec(memory_space=pltpu.VMEM)
    there = pl.BlockSpec(memory_space=pl.ANY)
    moved = sum(v.size * v.dtype.itemsize for v in operands) + sum(v.size * v.dtype.itemsize for v in outs.values())
    results = pl.pallas_call(
        kernel,
        out_shape=list(outs.values()),
        in_specs=[pl.BlockSpec(memory_space=pltpu.SMEM)] + [here] * n_small + [there] * (len(operands) - n_small),
        out_specs=[there] * len(outs),
        scratch_shapes=[pltpu.VMEM(*pair) for pair in scratch.values()] + [pltpu.SemaphoreType.DMA((copies,))],
        compiler_params=pltpu.CompilerParams(vmem_limit_bytes=VMEM),
        cost_estimate=pl.CostEstimate(flops=us * FLOPS_PER_US, bytes_accessed=moved // 4, transcendentals=0),
    )(sel, *operands)
    return types.SimpleNamespace(**dict(zip(outs, results)))


def norm_parts(values):
    center = values - jnp.mean(values, axis=-1, keepdims=True)
    inverse = lax.rsqrt(jnp.mean(center * center, axis=-1, keepdims=True) + eps_norm)
    return center * inverse, inverse


def norm_back(grad, values, gain):
    normed, inverse = norm_parts(values)
    scaled = grad * gain
    result = inverse * (
        scaled
        - jnp.mean(scaled, axis=-1, keepdims=True)
        - normed * jnp.mean(scaled * normed, axis=-1, keepdims=True)
    )
    return result, jnp.sum(grad * normed, axis=0, keepdims=True), jnp.sum(grad, axis=0, keepdims=True)


def gelu_parts(hidden):
    size = jnp.abs(hidden)
    bell = jnp.exp(hidden * hidden * -0.5)
    t = 1.0 / (1.0 + size * (0.3275911 * 0.7071067811865476))
    poly = 0.5 * 1.061405429 * t + 0.5 * -1.453152027
    poly = poly * t + 0.5 * 1.421413741
    poly = poly * t + 0.5 * -0.284496736
    poly = poly * t + 0.5 * 0.254829592
    tail = poly * t * bell
    active = jnp.maximum(hidden, 0.0) - size * tail
    share = jnp.where(hidden >= 0.0, 1.0 - tail, tail)
    return active, share + hidden * (bell * 0.3989422804014327)


def column_of(row):
    return jnp.transpose(jnp.broadcast_to(row, (128, row.shape[1])))[:, :1]


def own_row(r, ref):
    return ref[pl.ds(r.sel[1], 1), :]


def embedded(r, base):
    r.tab[...] = jnp.zeros_like(r.tab)
    r.tab[: r.table.shape[0], :] = r.table[...]
    high = r.tab[...].astype(bf16)
    low = (r.tab[...] - high.astype(f32)).astype(bf16)
    place = column_of(own_row(r, r.pos).astype(f32))
    lanes = lax.broadcasted_iota(jnp.int32, (base.shape[0], r.tab.shape[0]), 1).astype(f32)
    hot = (place == lanes).astype(bf16)
    return base[...].astype(f32) + (dot(hot, high) + dot(hot, low))


def attention_half(r, loads, gains, shifts):
    width = r.u.shape[1]
    id_row = own_row(r, r.ids).astype(f32)
    r.bias[...] = jnp.where(column_of(id_row) == id_row, 0.0, neg_large)
    r.put(r.u, r.u_o)
    normed, _ = norm_parts(r.u[...])
    r.attn_in[...] = (normed * gains[0:1, :] + shifts[0:1, :]).astype(bf16)
    r.put(r.attn_in, r.attn_in_o)
    for part in range(3):
        loads[part].wait()
        cols = slice(part * width, (part + 1) * width)
        value = dot(r.attn_in[...], r.v_qkv[:, cols])
        if part != 1:
            value = value + shifts[1 + part // 2 : 2 + part // 2, :]
        r.qkv[:, cols] = value.astype(bf16)
    r.put(r.qkv, r.qkv_o)
    lane = lax.broadcasted_iota(jnp.int32, (1, PAIR), 1)
    for pair in range(width // PAIR):
        lo = pair * PAIR
        q2 = r.qkv[:, lo : lo + PAIR] * 0.125
        k2 = r.qkv[:, width + lo : width + lo + PAIR]
        v2 = r.qkv[:, 2 * width + lo : 2 * width + lo + PAIR]
        total = None
        for side in range(2):
            mine = (lane < HEAD) if side == 0 else (lane >= HEAD)
            scores = dot(jnp.where(mine, q2, 0), k2, NT) + r.bias[...]
            peak = jnp.max(scores, axis=-1, keepdims=True)
            grown = jnp.exp(scores - peak)
            grown = (grown * (1.0 / jnp.sum(grown, axis=-1, keepdims=True))).astype(bf16)
            r.probs[2 * pair + side] = grown
            term = dot(grown, jnp.where(mine, v2, 0))
            total = term if total is None else total + term
        r.context[:, lo : lo + PAIR] = total.astype(bf16)
        r.put(r.probs.at[2 * pair : 2 * pair + 2], r.probs_o.at[2 * pair : 2 * pair + 2])
    r.put(r.context, r.context_o)
    loads[3].wait()
    r.residual[...] = r.u[...] + (dot(r.context[...], r.v_out[...]) + shifts[3:4, :])
    r.put(r.residual, r.residual_o)
    normed, _ = norm_parts(r.residual[...])
    r.mlp_in[...] = (normed * gains[1:2, :] + shifts[4:5, :]).astype(bf16)
    r.put(r.mlp_in, r.mlp_in_o)


def widen(r, mlp_in, weight, loads, b_fc1, active, slope, active_o, slope_o):
    part = active.shape[1] // len(loads)
    for start in range(0, active.shape[1], TILE):
        if start % part == 0:
            loads[start // part].wait()
        cols = slice(start, start + TILE)
        act, incline = gelu_parts(dot(mlp_in[...], weight[:, cols]) + b_fc1[:, cols])
        active[:, cols] = act.astype(bf16)
        slope[:, cols] = incline.astype(bf16)
    r.put(active, active_o)
    r.put(slope, slope_o)


def stack_columns(r, left, right, part, begin, total):
    side = 1 - r.sel[1]
    height, step = left.shape[1], part.shape[1]
    for index in range(total // step):
        cols = pl.ds(pl.multiple_of(side * total + index * step, 128), step)
        spot = begin + index * height
        part[spot : spot + height, :] = dot(left[...], right[:, cols], TN).astype(bf16)


def half_of(side, width):
    return pl.ds(pl.multiple_of(side * width, 128), width)


def away(r, left, right, part, part_o):
    half = part.shape[1]
    part[...] = dot(left[...], right[:, half_of(1 - r.sel[1], half)], TN).astype(bf16)
    r.put(part, part_o)


def stream_shapes(jobs, block):
    first = ((jobs, 8) + block, bf16)
    second = ((jobs, 4, 2) + block, bf16)
    return dict(away_p=first, kept_p=first, away_q=second, kept_q=second)


def stream_scratch(jobs, block):
    return dict(held_p=((jobs, 8, 2) + block, bf16), held_q=((jobs, 4, 2, 2) + block, bf16))


def canonical(total, tall):
    rows, columns = total.shape
    if tall:
        blocks = total.reshape(16, rows // 16, columns)
        middle = rows // 32
        return blocks[:, :middle], blocks[:, middle:]
    quarter = columns // 4
    parts = [total[:, i * quarter : (i + 1) * quarter].reshape(16, rows // 16, quarter) for i in range(4)]
    return jnp.concatenate(parts[:2], axis=1), jnp.concatenate(parts[2:], axis=1)


def emit(r, job, total, tall, extra=None):
    first, second = canonical(total, tall)
    if extra is not None:
        first = jnp.concatenate([first, extra[:, :32]], axis=1)
        second = jnp.concatenate([second, extra[:, 32:]], axis=1)
    place = r.sel[2]
    x, y = place % 2, place // 2 % 2
    block = r.held_p.shape[-2:]
    r.held_p[job] = first.astype(bf16).reshape((8, 2) + block)
    r.held_q[job] = second.astype(bf16).reshape((4, 2, 2) + block)
    r.put(r.held_p.at[job, :, 1 - x], r.away_p.at[job])
    r.put(r.held_p.at[job, :, x], r.kept_p.at[job])
    r.put(r.held_q.at[job, :, 1 - y], r.away_q.at[job])
    r.put(r.held_q.at[job, :, y], r.kept_q.at[job])


def hop(sel, tasks, after=()):
    large, outs, scratch, plans = {}, {}, {}, []

    def name(kind, index, stream):
        return kind + str(2 * index + stream)

    for index, (step, kept, came) in enumerate(tasks):
        jobs = kept[0].shape[0]
        block = kept[0].shape[-2:]
        if step == 2:
            whole = [(jobs, 2, 2, 2) + block] * 2
            cut = [(jobs, 2, 2, 2) + block]
        elif step == 3:
            whole = [(jobs, 2, 2, 2) + block]
            cut = [(jobs, 2) + block] * 2
        elif step == 4:
            whole = [(jobs, 2) + block] * 2
            cut = [(jobs, 2) + block]
        else:
            whole = [(jobs, 2) + block]
            cut = []
        for stream, dims in enumerate(whole):
            large[name("k", index, stream)] = kept[stream].reshape(dims)
            large[name("c", index, stream)] = came[stream].reshape(dims)
            scratch[name("a", index, stream)] = (dims, bf16)
            scratch[name("b", index, stream)] = (dims, bf16)
        for stream, dims in enumerate(cut):
            outs[name("s", index, stream)] = struct((dims, bf16))
            outs[name("t", index, stream)] = struct((dims, bf16))
        if step == 5:
            outs[name("t", index, 0)] = struct((whole[0], bf16))
        plans.append((step, len(whole)))

    def body(r):
        place = r.sel[2]
        x, y, z0, z1 = place % 2, place // 2 % 2, place // 4 % 2, place // 8
        ref = lambda kind, index, stream=0: getattr(r, name(kind, index, stream))
        waits = []
        for index, (step, streams) in enumerate(plans):
            for stream in range(streams):
                waits.append(r.get(ref("k", index, stream), ref("a", index, stream)))
                waits.append(r.get(ref("c", index, stream), ref("b", index, stream)))
        for index, (step, streams) in enumerate(plans):
            for stream in range(streams):
                waits.pop(0).wait()
                waits.pop(0).wait()
                a, b = ref("a", index, stream), ref("b", index, stream)
                a[...] = (a[...].astype(f32) + b[...].astype(f32)).astype(bf16)
                if step == 2:
                    r.put(a.at[:, :, 1 - z0], ref("s", index).at[:, stream])
                    r.put(a.at[:, :, z0], ref("t", index).at[:, stream])
                elif step == 3:
                    for way, bit in ((0, y), (1, x)):
                        r.put(a.at[:, way, :, 1 - bit], ref("s", index, way))
                        r.put(a.at[:, way, :, bit], ref("t", index, way))
                elif step == 4:
                    r.put(a.at[:, 1 - z1], ref("s", index).at[:, stream])
                    r.put(a.at[:, z1], ref("t", index).at[:, stream])
                else:
                    r.put(a, ref("t", index))

    got = call(body, 3, sel, {}, large, outs, scratch, 64, after)
    results = []
    for index, (step, streams) in enumerate(plans):
        count = 2 if step == 3 else 1
        sent = [getattr(got, name("s", index, i)) for i in range(count)] if step < 5 else []
        results.append((sent, [getattr(got, name("t", index, i)) for i in range(count)]))
    return results


def swap(array):
    return lax.ppermute(array, "section", [(0, 1), (1, 0)])


def across(array, bit):
    count = lax.axis_size("dp")
    return lax.ppermute(array, "dp", [(i, i ^ (1 << bit)) for i in range(count)])


def scatter_blocks(blocks, order):
    count = blocks.shape[0]
    bits = count.bit_length() - 1
    rest = blocks.shape[1:]
    place = lax.axis_index("dp")
    held = blocks.reshape((2,) * bits + rest)
    left = list(reversed(range(bits)))
    for bit in order:
        dim = left.index(bit)
        mine = (place >> bit) & 1
        sent = lax.dynamic_index_in_dim(held, 1 - mine, dim, keepdims=False)
        kept = lax.dynamic_index_in_dim(held, mine, dim, keepdims=False)
        held = (kept.astype(f32) + across(sent, bit).astype(f32)).astype(blocks.dtype)
        left.remove(bit)
    return held


def per_device(
    patches, pos_table, pos_index, image_ids, ln_gains, biases, w_qkv, w_out, w_fc1, b_fc1, w_fc2, cotangent
):
    section = lax.axis_index("section")
    place = lax.axis_index("dp")
    count = lax.axis_size("dp")
    lead = section == 0
    rows, width = patches.shape[1:]
    ff = w_fc1.shape[2]
    half, heads = width // 2, width // HEAD
    fast = count == 16 and (width // count) % 16 == 0 and (ff // count) % 32 == 0 and width % 256 == 0
    block = (ff // 32, half)

    tokens, tokens32 = ((rows, width), bf16), ((rows, width), f32)
    triple, wide = ((rows, 3 * width), bf16), ((rows, ff), bf16)
    probs_t = ((heads, rows, rows), bf16)
    lines = ((8, width), f32)
    t_qkv, t_out, t_fc1, t_fc2 = ((width, 3 * width), bf16), ((width, width), bf16), ((width, ff), bf16), ((ff, width), bf16)
    half_fc2, half_fc1 = ((ff, half), bf16), ((width, ff // 2), bf16)

    def outputs(**pairs):
        return {name: struct(pair) for name, pair in pairs.items()}

    sel = [
        jnp.stack([(section == layer).astype(jnp.int32), section.astype(jnp.int32), place.astype(jnp.int32)])
        for layer in range(2)
    ]
    gains, shifts, b_fc1 = [(item, swap(item)) for item in (ln_gains[0], biases[0], b_fc1)]
    qkv_w = (w_qkv[0], swap(w_qkv[0]))
    out_w = (w_out[0], swap(w_out[0]))
    fc1_w = (w_fc1[0], swap(w_fc1[0]))
    fc2_w = (w_fc2[0], swap(w_fc2[0]))
    grad = cotangent[0]

    kept_out = dict(u_o=tokens32, attn_in_o=tokens, qkv_o=triple, probs_o=probs_t, context_o=tokens, residual_o=tokens32,
                    mlp_in_o=tokens)
    kept_scratch = dict(u=tokens32, attn_in=tokens, qkv=triple, probs=probs_t, context=tokens, residual=tokens32,
                        mlp_in=tokens, bias=((rows, rows), f32), v_qkv=t_qkv, v_out=t_out)

    def first_half(r):
        first = r.get(r.base, r.base_v)
        loads = r.pieces(r.w_qkv, r.v_qkv, 3, 1) + [r.pick(r.w_out, r.v_out)]
        first.wait()
        r.u[...] = embedded(r, r.base_v)
        attention_half(r, loads, r.either(r.gains), r.either(r.shifts))

    kept0 = call(
        first_half, 11, sel[0],
        dict(ids=image_ids, pos=pos_index, table=pos_table, gains=gains, shifts=shifts),
        dict(base=patches[0], w_qkv=qkv_w, w_out=out_w),
        outputs(**kept_out),
        dict(base_v=tokens, tab=((256, width), f32), **kept_scratch),
    )

    def second_half(r):
        early = r.get(r.mlp_in0_h, r.mlp_in0)
        wide0 = r.pieces(r.w_fc1, r.v_fc1, 4, 1)
        other = lambda pair: (pair[1], pair[0])
        early.wait()
        narrow0 = [r.pick(r.w_fc2, r.v_fc2), r.get(r.residual0_h, r.residual0)]
        loads = r.pieces(other(r.w_qkv), r.v_qkv, 3, 1) + [r.pick(other(r.w_out), r.v_out)]
        widen(r, r.mlp_in0, r.v_fc1, wide0, r.either(r.b_fc1), r.active0, r.slope0, r.active0_o, r.slope0_o)
        for copy in narrow0:
            copy.wait()
        shifts0 = r.either(r.shifts)
        middle = r.residual0[...] + (dot(r.active0[...], r.v_fc2[...]) + shifts0[5:6, :])
        r.u[...] = middle.astype(bf16).astype(f32)
        wide1 = [r.pick(other(r.w_fc1), r.v_fc1b)]
        late = r.get(r.grad_h, r.grad)
        attention_half(r, loads, r.either(other(r.gains)), r.either(other(r.shifts)))
        widen(r, r.mlp_in, r.v_fc1b, wide1, r.either(other(r.b_fc1)), r.active, r.slope, r.active_o, r.slope_o)
        late.wait()
        away(r, r.active, r.grad, r.part, r.part_o)

    kept1 = call(
        second_half, 28, sel[0],
        dict(ids=image_ids, gains=gains, shifts=shifts, b_fc1=b_fc1),
        dict(mlp_in0_h=kept0.mlp_in_o, residual0_h=kept0.residual_o, grad_h=grad,
             w_qkv=qkv_w, w_out=out_w, w_fc1=fc1_w, w_fc2=fc2_w),
        outputs(active0_o=wide, slope0_o=wide, active_o=wide, slope_o=wide, part_o=half_fc2, **kept_out),
        dict(mlp_in0=tokens, residual0=tokens32, active0=wide, slope0=wide, active=wide, slope=wide, grad=tokens,
             part=half_fc2, v_fc1=t_fc1, v_fc1b=t_fc1, v_fc2=t_fc2, **kept_scratch),
    )
    kept0.active_o, kept0.slope_o = kept1.active0_o, kept1.slope0_o
    kept = [kept0, kept1]


    def mlp_back(layer, grad, after=()):
        last = layer == 1

        def body(r):
            first = r.get(r.grad_h, r.grad)
            quarter = ff // 4
            weight = r.pieces(r.w_fc2, r.v_fc2, 4, 0)
            inclines = r.pieces([r.slope_h, r.slope_h], r.slope, 4, 1)
            first.wait()
            later = [r.get(r.mlp_in_h, r.mlp_in)]
            if last:
                later += [r.get(r.active_h, r.active), r.get(r.residual_h, r.residual)]
            r.col[...] = jnp.sum(r.grad[...].astype(f32), axis=0, keepdims=True)
            r.put(r.col, r.b_fc2_o)
            for start in range(0, ff, TILE):
                if start % quarter == 0:
                    weight[start // quarter].wait()
                    inclines[start // quarter].wait()
                cols = slice(start, start + TILE)
                inner = (dot(r.grad[...], r.v_fc2[cols, :], NT) * r.slope[:, cols].astype(f32)).astype(bf16)
                r.grad_hidden[:, cols] = inner
                r.row[:, cols] = jnp.sum(inner.astype(f32), axis=0, keepdims=True)
            r.put(r.grad_hidden, r.grad_hidden_o)
            r.put(r.row, r.b_fc1_o)
            later[0].wait()
            away(r, r.mlp_in, r.grad_hidden, r.part, r.part_o)
            if last:
                later[1].wait()
                later[2].wait()
                result = r.residual[...] + (dot(r.active[...], r.v_fc2[...]) + r.either(r.shifts)[5:6, :])
                r.x_out[...] = result.astype(bf16)
                r.put(r.x_out, r.x_o)

        have = kept[layer]
        large = dict(grad_h=grad, slope_h=have.slope_o, mlp_in_h=have.mlp_in_o, w_fc2=fc2_w)
        outs = dict(grad_hidden_o=wide, part_o=half_fc1, b_fc1_o=((1, ff), f32), b_fc2_o=((1, width), f32))
        scratch = dict(grad=tokens, slope=wide, mlp_in=tokens, v_fc2=t_fc2, grad_hidden=wide, part=half_fc1,
                       row=((1, ff), f32), col=((1, width), f32))
        small = {}
        if last:
            large |= dict(active_h=have.active_o, residual_h=have.residual_o)
            scratch |= dict(active=wide, residual=tokens32, x_out=tokens)
            outs |= dict(x_o=tokens)
            small = dict(shifts=shifts)
        return call(body, 10, sel[layer], small, large, outputs(**outs), scratch, after=after)

    def finish(r, job, flat_o, flat, total, tall, extra=None):
        if fast:
            emit(r, job, total, tall, extra)
        else:
            flat[...] = total.astype(bf16)
            r.put(flat, flat_o)

    def rest_total(r):
        came = [r.came_rest[i * width : (i + 1) * width, :].astype(f32) for i in range(4)]
        own = dot(r.attn_in[...], r.grad_qkv[:, half_of(r.sel[1], 3 * half)], TN)
        side = dot(r.p_context[...], r.p_branch[:, half_of(r.sel[1], half)], TN)
        return jnp.concatenate([own, side], axis=1) + jnp.concatenate(came, axis=1)

    def rest_operands(layer, mid, att, came):
        return (
            dict(attn_in_h=kept[layer].attn_in_o, grad_qkv_h=att.grad_qkv_o, came_rest_h=came,
                 p_context_h=kept[layer].context_o, p_branch_h=mid.grad_branch_o),
            dict(attn_in=tokens, grad_qkv=triple, came_rest=((4 * width, half), bf16), p_context=tokens, p_branch=tokens),
        )

    def rest_loads(r):
        return [r.get(r.attn_in_h, r.attn_in), r.get(r.grad_qkv_h, r.grad_qkv), r.get(r.p_context_h, r.p_context),
                r.get(r.p_branch_h, r.p_branch), r.get(r.came_rest_h.at[: 4 * width], r.came_rest)]

    def sum_specs(jobs, flats, more=0):
        if fast:
            taller = (block[0] + more, block[1])
            return stream_shapes(jobs, taller), stream_scratch(jobs, taller)
        return flats, {name + "_v": pair for name, pair in flats.items()}

    def middle_back(layer, grad, mlp, came_fc2, before, after=()):
        def body(r):
            first = r.pieces([r.grad_hidden_h, r.grad_hidden_h], r.grad_hidden, 4, 1)
            weight = r.pieces(r.w_fc1, r.v_fc1, 4, 1)
            second = [r.get(r.grad_h, r.grad), r.get(r.residual_h, r.residual)]
            out_weight = r.pick(r.w_out, r.v_out)
            gains1 = r.either(r.gains)[1:2, :]
            d_in = None
            for index in range(4):
                first[index].wait()
                weight[index].wait()
                cols = slice(index * ff // 4, (index + 1) * ff // 4)
                term = dot(r.grad_hidden[:, cols], r.v_fc1[:, cols], NT)
                d_in = term if d_in is None else d_in + term
                if index == 0:
                    fourth = [r.get(r.active_h, r.active), r.get(r.came_fc2_h.at[came_fc2.shape[0] - ff :], r.came_fc2)]
                    fifth = rest_loads(r) if before else []
            for copy in second:
                copy.wait()
            back, d_gain, d_shift = norm_back(d_in, r.residual[...], gains1)
            r.grad_res[...] = r.grad[...].astype(f32) + back
            r.grad_branch[...] = r.grad_res[...].astype(bf16)
            r.put(r.grad_res, r.grad_res_o)
            r.put(r.grad_branch, r.grad_branch_o)
            r.lines[...] = jnp.zeros_like(r.lines)
            r.lines[0:1, :] = d_gain
            r.lines[1:2, :] = d_shift
            r.lines[2:3, :] = jnp.sum(r.grad_branch[...].astype(f32), axis=0, keepdims=True)
            r.put(r.lines, r.lines_o)
            out_weight.wait()
            r.grad_context[...] = dot(r.grad_branch[...], r.v_out[...], NT).astype(bf16)
            r.put(r.grad_context, r.grad_context_o)
            for copy in fourth:
                copy.wait()
            total = dot(r.active[...], r.grad[:, half_of(r.sel[1], half)], TN) + r.came_fc2[...].astype(f32)
            finish(r, 0, *((r.f2, r.f2_v) if not fast else (None, None)), total, True)
            if before:
                for copy in fifth:
                    copy.wait()
                finish(r, 1, *((r.fr, r.fr_v) if not fast else (None, None)), rest_total(r), False)

        have = kept[layer]
        large = dict(grad_hidden_h=mlp.grad_hidden_o, grad_h=grad, residual_h=have.residual_o,
                     active_h=have.active_o, came_fc2_h=came_fc2, w_fc1=fc1_w, w_out=out_w)
        scratch = dict(grad_hidden=wide, grad=tokens, residual=tokens32, active=wide, came_fc2=half_fc2,
                       v_fc1=t_fc1, v_out=t_out, grad_res=tokens32, grad_branch=tokens, grad_context=tokens, lines=lines)
        outs = dict(grad_res_o=tokens32, grad_branch_o=tokens, grad_context_o=tokens, lines_o=lines)
        flats = dict(f2=half_fc2)
        if before:
            more, space = rest_operands(*before)
            large |= more
            scratch |= space
            flats |= dict(fr=half_fc1)
        more, space = sum_specs(2 if before else 1, flats)
        return call(body, 16 if before else 13, sel[layer], dict(gains=gains), large, outputs(**outs, **more), scratch | space,
                    after=after)

    def attention_back(layer, mlp, mid, came_fc1, next_active, after=()):
        table_rows = -(-pos_table.shape[0] // 128) * 128
        bottom = layer == 0

        def body(r):
            first = [r.get(r.grad_context_h, r.grad_context), r.get(r.qkv_h, r.qkv), r.get(r.context_h, r.context)]
            fetch = lambda begin, end: [r.get(r.probs_h.at[head], r.probs.at[head]) for head in range(begin, end)]
            ready = fetch(0, 4)
            for copy in first:
                copy.wait()
            lane = lax.broadcasted_iota(jnp.int32, (1, PAIR), 1)
            for pair in range(heads // 2):
                if pair == 0:
                    ready += fetch(4, heads)
                    second = [r.get(r.attn_in_h, r.attn_in), r.get(r.grad_branch_h, r.grad_branch)]
                    weight = r.pick(r.w_qkv, r.v_qkv)
                    third = [r.get(r.grad_res_h, r.grad_res), r.get(r.u_h, r.u)]
                    fourth = [r.get(r.mlp_in_h, r.mlp_in), r.get(r.grad_hidden_h, r.grad_hidden),
                              r.get(r.came_fc1_h, r.came_fc1)]
                    if not bottom:
                        fifth = r.get(r.active_h, r.active)
                lo = pair * PAIR
                q2 = r.qkv[:, lo : lo + PAIR] * 0.125
                k2 = r.qkv[:, width + lo : width + lo + PAIR]
                v2 = r.qkv[:, 2 * width + lo : 2 * width + lo + PAIR]
                out2 = r.grad_context[:, lo : lo + PAIR]
                meet = out2.astype(f32) * r.context[:, lo : lo + PAIR].astype(f32)
                sums = [None, None, None]
                for side in range(2):
                    mine = (lane < HEAD) if side == 0 else (lane >= HEAD)
                    ready[2 * pair + side].wait()
                    prob = r.probs[2 * pair + side]
                    out_h = jnp.where(mine, out2, 0)
                    shared = jnp.sum(jnp.where(mine, meet, 0.0), axis=-1, keepdims=True)
                    d_score = (prob.astype(f32) * (dot(out_h, v2, NT) - shared)).astype(bf16)
                    terms = [
                        dot(d_score, jnp.where(mine, k2, 0)) * 0.125,
                        dot(d_score, jnp.where(mine, q2, 0), TN),
                        dot(prob, out_h, TN),
                    ]
                    sums = [term if old is None else old + term for old, term in zip(sums, terms)]
                for part in range(3):
                    r.grad_qkv[:, part * width + lo : part * width + lo + PAIR] = sums[part].astype(bf16)
            r.put(r.grad_qkv, r.grad_qkv_o)
            for copy in second:
                copy.wait()
            stack_columns(r, r.attn_in, r.grad_qkv, r.part, 0, 3 * half)
            stack_columns(r, r.context, r.grad_branch, r.part, 3 * width, half)
            if bottom:
                r.put(r.part, r.part_o)
            else:
                r.put(r.part.at[: 4 * width], r.part_o.at[: 4 * width])
            weight.wait()
            d_in = dot(r.grad_qkv[...], r.v_qkv[...], NT)
            for copy in third:
                copy.wait()
            back, d_gain, d_shift = norm_back(d_in, r.u[...], r.either(r.gains)[0:1, :])
            down = r.grad_res[...] + back
            r.x_out[...] = down.astype(bf16)
            r.put(r.x_out, r.x_o)
            r.lines[...] = jnp.zeros_like(r.lines)
            r.lines[0:1, :] = d_gain
            r.lines[1:2, :] = d_shift
            for row, part in ((2, 0), (3, 2)):
                cols = slice(part * width, (part + 1) * width)
                r.lines[row : row + 1, :] = jnp.sum(r.grad_qkv[:, cols].astype(f32), axis=0, keepdims=True)
            r.put(r.lines, r.lines_o)
            if bottom:
                spot = lax.broadcasted_iota(jnp.int32, (table_rows, rows), 0)
                hot = (spot == own_row(r, r.pos)).astype(bf16)
                low = (down - r.x_out[...].astype(f32)).astype(bf16)
                across_rows = (((0,), (1,)), ((), ()))
                r.tab[...] = dot(r.x_out[...], hot, across_rows) + dot(low, hot, across_rows)
                r.put(r.tab, r.tab_o)
            else:
                fifth.wait()
                stack_columns(r, r.active, r.x_out, r.part, 4 * width, half)
                r.put(r.part.at[4 * width :], r.part_o.at[4 * width :])
            for copy in fourth:
                copy.wait()
            own = r.grad_hidden[:, half_of(r.sel[1], ff // 2)]
            total = dot(r.mlp_in[...], own, TN) + r.came_fc1[...].astype(f32)
            finish(r, 0, *((r.f1, r.f1_v) if not fast else (None, None)), total, False)

        have = kept[layer]
        large = dict(grad_context_h=mid.grad_context_o, qkv_h=have.qkv_o, probs_h=have.probs_o, context_h=have.context_o,
                     grad_res_h=mid.grad_res_o, u_h=have.u_o, attn_in_h=have.attn_in_o, mlp_in_h=have.mlp_in_o,
                     grad_hidden_h=mlp.grad_hidden_o, came_fc1_h=came_fc1, grad_branch_h=mid.grad_branch_o, w_qkv=qkv_w)
        half_rest = ((4 * width if bottom else 4 * width + ff, half), bf16)
        scratch = dict(grad_context=tokens, qkv=triple, probs=probs_t, context=tokens, grad_res=tokens32, u=tokens32,
                       attn_in=tokens, mlp_in=tokens, grad_hidden=wide, came_fc1=half_fc1, v_qkv=t_qkv, grad_qkv=triple,
                       x_out=tokens, part=half_rest, grad_branch=tokens, lines=lines)
        outs = dict(part_o=half_rest, grad_qkv_o=triple, x_o=tokens, lines_o=lines)
        small = dict(gains=gains)
        if bottom:
            small |= dict(pos=pos_index)
            scratch |= dict(tab=((width, table_rows), f32))
            outs |= dict(tab_o=((width, table_rows), f32))
        else:
            large |= dict(active_h=next_active)
            scratch |= dict(active=wide)
        more, space = sum_specs(1, dict(f1=half_fc1))
        return call(body, 24, sel[layer], small, large, outputs(**outs, **more), scratch | space, 60, after)

    def rest_sum(*before, extra=None, after=()):
        def body(r):
            loads = rest_loads(r)
            if fast:
                loads += [r.get(r.extra_h, r.extra)]
            for copy in loads:
                copy.wait()
            more = r.extra[...].astype(f32) if fast else None
            finish(r, 0, *((r.fr, r.fr_v) if not fast else (None, None)), rest_total(r), False, more)

        large, scratch = rest_operands(*before)
        if fast:
            large |= dict(extra_h=extra)
            scratch |= dict(extra=(extra.shape, bf16))
        more, space = sum_specs(1, dict(fr=half_fc1), 32)
        return call(body, 6, sel[0], {}, large, outputs(**more), scratch | space, after=after)


    def begin(got):
        return [across(got.away_p, 0), across(got.away_q, 1)], [got.kept_p, got.kept_q]

    def onward(step, result):
        sent, stay = result
        bits = {2: (2,), 3: (1, 0), 4: (3,)}[step]
        return [across(piece, bit) for piece, bit in zip(sent, bits)], stay

    def narrow_rows(mlp, mid, att):
        stack = jnp.concatenate(
            [att.lines_o[0:1], mid.lines_o[0:1], att.lines_o[1:4], mid.lines_o[2:3], mid.lines_o[1:2], mlp.b_fc2_o], axis=0
        )
        return stack.reshape(8, count, -1).transpose(1, 0, 2), mlp.b_fc1_o.reshape(count, -1)

    came_fc2 = swap(kept1.part_o)
    mlp1 = mlp_back(1, grad)
    out_tokens = mlp1.x_o
    came_fc1 = swap(mlp1.part_o)
    mid1 = middle_back(1, grad, mlp1, came_fc2, None)
    if fast:
        a_came, a_kept = begin(mid1)
    att1 = attention_back(1, mlp1, mid1, came_fc1, kept0.active_o)
    came_rest1 = swap(att1.part_o)
    middle_grad = att1.x_o
    wait = ()
    if fast:
        b_came, b_kept = begin(att1)
        (a_sent,) = hop(sel[0], [(2, a_kept, a_came)], [middle_grad])
        a_came, a_kept = onward(2, a_sent)
        wait = a_sent[1]
    mlp0 = mlp_back(0, middle_grad, wait)
    came_fc1 = swap(mlp0.part_o)
    if fast:
        a_sent, b_sent = hop(sel[0], [(3, a_kept, a_came), (2, b_kept, b_came)], [mlp0.part_o])
        a_came, a_kept = onward(3, a_sent)
        b_came, b_kept = onward(2, b_sent)
        wait = b_sent[1]
    mid0 = middle_back(0, middle_grad, mlp0, came_rest1, (1, mid1, att1, came_rest1), wait)
    if fast:
        c_came, c_kept = begin(mid0)
        a_sent, b_sent = hop(sel[0], [(4, a_kept, a_came), (3, b_kept, b_came)], [mid0.grad_res_o])
        a_came, a_kept = onward(4, a_sent)
        b_came, b_kept = onward(3, b_sent)
        wait = b_sent[1]
    att0 = attention_back(0, mlp0, mid0, came_fc1, None, wait)
    came_rest0 = swap(att0.part_o)
    grad_patches = att0.x_o
    vectors = [narrow_rows(mlp0, mid0, att0), narrow_rows(mlp1, mid1, att1)]
    table = att0.tab_o.reshape(2, count, -1, att0.tab_o.shape[1])
    table_rows = pos_table.shape[0]
    columns = width // count
    if fast:
        d_came, d_kept = begin(att0)
        a_sent, b_sent, c_sent = hop(
            sel[0], [(5, a_kept, a_came), (4, b_kept, b_came), (2, c_kept, c_came)], [grad_patches]
        )
        fc2_1 = a_sent[1][0][0]
        b_came, b_kept = onward(4, b_sent)
        c_came, c_kept = onward(2, c_sent)

        def small_block(layer):
            rows8, wide_row = vectors[layer]
            upper = jnp.pad(table[layer], ((0, 0), (0, 0), (0, half - table.shape[3])))
            lower = jnp.pad(rows8, ((0, 0), (0, 0), (0, 128 - columns)))
            side = jnp.pad(wide_row[:, None, :], ((0, 0), (0, 7), (0, half - 128 - wide_row.shape[1])))
            lower = jnp.concatenate([lower, side], axis=2)
            return jnp.concatenate([upper, lower], axis=1)

        extra = jnp.concatenate([small_block(layer) for layer in range(2)], axis=1).astype(bf16)
        rest0 = rest_sum(0, mid0, att0, came_rest0, extra=extra, after=c_sent[1])
        e_came, e_kept = begin(rest0)
        b_sent, c_sent, d_sent = hop(
            sel[0], [(5, b_kept, b_came), (3, c_kept, c_came), (2, d_kept, d_came)], [rest0.kept_p]
        )
        fc1_1 = b_sent[1][0][0]
        c_came, c_kept = onward(3, c_sent)
        d_came, d_kept = onward(2, d_sent)
        c_sent, d_sent, e_sent = hop(sel[0], [(4, c_kept, c_came), (3, d_kept, d_came), (2, e_kept, e_came)])
        c_came, c_kept = onward(4, c_sent)
        d_came, d_kept = onward(3, d_sent)
        e_came, e_kept = onward(2, e_sent)
        c_sent, d_sent, e_sent = hop(sel[0], [(5, c_kept, c_came), (4, d_kept, d_came), (3, e_kept, e_came)])
        fc2_0, rest_1 = c_sent[1][0][0], c_sent[1][0][1]
        d_came, d_kept = onward(4, d_sent)
        e_came, e_kept = onward(3, e_sent)
        d_sent, e_sent = hop(sel[0], [(5, d_kept, d_came), (4, e_kept, e_came)])
        fc1_0 = d_sent[1][0][0]
        e_came, e_kept = onward(4, e_sent)
        (e_sent,) = hop(sel[0], [(5, e_kept, e_came)])
        rest_0 = e_sent[1][0][0]
        both = rest_0[:, block[0] :]
        small = jnp.where(lead, both[0], both[1]).astype(f32) + swap(jnp.where(lead, both[1], both[0])).astype(f32)
        rest_0 = rest_0[:, : block[0]]
        part = 24
        grad_table = small[:part, :table_rows].T
        grad_vectors = small[part:, :columns]
        grad_b_fc1 = small[part, 128 : 128 + ff // count]

        def flat_block(piece):
            return piece.reshape(4, -1, half).transpose(1, 0, 2).reshape(-1, 4 * half)

        own = [
            [fc2_0.reshape(-1, half), flat_block(fc1_0), flat_block(rest_0)],
            [fc2_1.reshape(-1, half), flat_block(fc1_1), flat_block(rest_1)],
        ]
    else:
        rest0 = rest_sum(0, mid0, att0, came_rest0)
        order = list(range(count.bit_length() - 1))
        spread = lambda total: scatter_blocks(total.reshape(count, -1, total.shape[1]), order)
        own = [
            [spread(mid0.f2), spread(att0.f1), spread(rest0.fr)],
            [spread(mid1.f2), spread(att1.f1), spread(mid0.fr)],
        ]
        both = [
            jnp.concatenate(
                [table[layer, :, :, :table_rows].reshape(count, -1), vectors[layer][0].reshape(count, -1), vectors[layer][1]],
                axis=1,
            )
            for layer in range(2)
        ]
        flat = scatter_blocks(jnp.where(lead, both[0], both[1]) + swap(jnp.where(lead, both[1], both[0])), order)
        size = table.shape[2] * table_rows
        grad_table = flat[:size].reshape(-1, table_rows).T
        grad_vectors = flat[size : size + 8 * columns].reshape(8, columns)
        grad_b_fc1 = flat[size + 8 * columns :]
    mine = [jnp.where(lead, first, second) for first, second in zip(*own)]
    came = [swap(jnp.where(lead, second, first)) for first, second in zip(*own)]
    lower = [jnp.where(lead, m, c).astype(f32) for m, c in zip(mine, came)]
    upper = [jnp.where(lead, c, m).astype(f32) for m, c in zip(mine, came)]
    wide_qkv = 3 * half
    grads = [
        jnp.concatenate([lower[2][:, :wide_qkv], upper[2][:, :wide_qkv]], axis=1),
        jnp.concatenate([lower[2][:, wide_qkv:], upper[2][:, wide_qkv:]], axis=1),
        jnp.concatenate([lower[1], upper[1]], axis=1),
        jnp.concatenate([lower[0], upper[0]], axis=1),
    ]
    return (
        out_tokens[None],
        grad_patches[None],
        grad_table,
        grad_vectors[:2][None],
        grad_vectors[2:][None],
        grads[0][None],
        grads[1][None],
        grads[2][None],
        grad_b_fc1[None],
        grads[3][None],
    )


def solution(mesh):
    placed = (
        P("section", "dp", None),
        P(),
        P(None, "dp"),
        P(None, "dp"),
        P("section", None, None),
        P("section", None, None),
        P("section", None, None),
        P("section", None, None),
        P("section", None, None),
        P("section", None),
        P("section", None, None),
        P("section", "dp", None),
    )
    return jax.shard_map(
        per_device,
        mesh=mesh,
        in_specs=placed,
        out_specs=(
            P("section", "dp", None),
            P("section", "dp", None),
            P(None, ("section", "dp")),
            P("section", None, "dp"),
            P("section", None, "dp"),
            P("section", "dp", None),
            P("section", "dp", None),
            P("section", "dp", None),
            P("section", "dp"),
            P("section", "dp", None),
        ),
        check_vma=False,
    )
```
